256 devices in a mesh: row: 16 (over x_lo, z), col: 4 (over y), ka: 4 (over x_hi, core).
Axes of the slice: x: 4 (x_hi: 2, x_lo: 2; x = x_hi * 2 + x_lo), y: 4, z: 8, core: 2. Of those that a mesh axis runs over, the one named last changes fastest.
Arguments:
- pair: bfloat16 [1024, 1024, 128], P('row', ('col', 'ka')), may hold values from -6 to 6
- in_gain: float32 [128], replicated, may hold values from 0.25 to 1.75
- in_shift: float32 [128], replicated, may hold values from -0.45 to 0.45
- w_inner: bfloat16 [128, 512], replicated, may hold values from -0.5 to 0.5
- inner_bias: float32 [512], replicated, may hold values from -3 to 3
- gate_weight: bfloat16 [128, 128], replicated, may hold values from -0.5 to 0.5
- gate_bias: float32 [128], replicated, may hold values from -3 to 3
- out_gain: float32 [128], replicated, may hold values from 0.25 to 1.75
- out_shift: float32 [128], replicated, may hold values from -3 to 3
- out_weight: bfloat16 [128, 128], replicated, may hold values from -0.5 to 0.5
- out_bias: float32 [128], replicated, may hold values from -3 to 3
Outputs:
- update: bfloat16 [1024, 1024, 128], P('row', ('col', 'ka'))
The draws below stay inside these ranges and needn't reach their ends.
All inputs are finite; a program needn't handle non-finite values.
Results may differ from the reference program's by a relative error of at most 0.014.
Values may be sent and summed in bfloat16 or wider, within the bound.
A program may use at most 192 MiB of HBM per device.

```python
import jax
import jax.numpy as jnp
from jax import lax

C = 128
H = 128
RESIDUES = 1024


def draw_inner_bias(key, part):
    key = jax.random.fold_in(key, 7)
    value_key, gate_key = jax.random.split(key)
    values = 0.05 * jax.random.truncated_normal(value_key, -3.0, 3.0, (4, H), jnp.float32)
    gates = jax.random.truncated_normal(gate_key, -3.0, 3.0, (4, H), jnp.float32)
    select = (jnp.arange(4) % 2 == 1)[:, None]
    return jnp.where(select, gates, values).reshape(4 * H).astype(jnp.float32)


def steps_of(stream_key, extent, pieces, low, top_value):
    level, own = 1.0, jax.random.fold_in(stream_key, 6)
    for axis_at, parts in pieces:
        steps = jnp.exp(jax.random.uniform(jax.random.fold_in(own, axis_at), (parts,), jnp.float32, low / len(pieces), top_value / len(pieces)))
        level = level * jnp.repeat(steps, extent[axis_at] // parts).reshape([-1 if axis == axis_at else 1 for axis in range(len(extent))])
    return level


def noise(rng, shape, deviation, reach, cuts=(), dtype=jnp.bfloat16):
    factor_of = steps_of(rng, shape, cuts, -0.22, 0.18) if cuts else 1.0
    values = jax.random.normal(rng, shape, jnp.float32) * deviation * factor_of
    return jnp.minimum(jnp.maximum(values, -reach), reach).astype(dtype)


def setup_inputs(seed: int = 0) -> dict:
    streams_of = jax.random.split(jax.random.key(seed), 12)
    pair = noise(streams_of[0], (RESIDUES, RESIDUES, C), 1.0, 6.0, ((0, 16), (1, 16)))
    in_gain = jnp.clip(1.0 + 0.15 * jax.random.normal(streams_of[1], (C,), jnp.float32), 0.25, 1.75)
    in_shift = noise(streams_of[2], (C,), 0.15, 0.45, (), jnp.float32)
    w_inner = noise(streams_of[3], (C, 4 * H), C ** -0.5, 0.5)
    inner_bias = draw_inner_bias(jax.random.fold_in(streams_of[11], 71), 0)
    gate_weight = noise(streams_of[5], (C, C), C ** -0.5, 0.5)
    gate_bias = noise(streams_of[6], (C,), 0.5, 3.0, (), jnp.float32)
    out_gain = jnp.clip(1.0 + 0.15 * jax.random.normal(streams_of[7], (H,), jnp.float32), 0.25, 1.75)
    out_shift = noise(streams_of[8], (H,), 0.5, 3.0, (), jnp.float32)
    out_weight = noise(streams_of[9], (H, C), H ** -0.5, 0.5)
    out_bias = noise(streams_of[10], (C,), 0.5, 3.0, (), jnp.float32)
    return dict(pair=pair, in_gain=in_gain, in_shift=in_shift, w_inner=w_inner, inner_bias=inner_bias, gate_weight=gate_weight, gate_bias=gate_bias, out_gain=out_gain, out_shift=out_shift, out_weight=out_weight, out_bias=out_bias)


def layer_norm(values, gain, shift):
    mean = lax.optimization_barrier(jnp.mean(values, axis=-1, keepdims=True))
    centred = values - mean
    variance = lax.optimization_barrier(jnp.mean(centred * centred, axis=-1, keepdims=True))
    return centred * lax.rsqrt(variance + 1e-05) * gain.astype(jnp.float32) + shift.astype(jnp.float32)

def reference(pair, in_gain, in_shift, w_inner, inner_bias, gate_weight, gate_bias, out_gain, out_shift, out_weight, out_bias):
    normed = layer_norm(pair.astype(jnp.float32), in_gain, in_shift).astype(jnp.bfloat16)
    flat = normed.reshape(RESIDUES * RESIDUES, C)
    inner = jnp.dot(flat, w_inner, preferred_element_type=jnp.float32) + inner_bias.astype(jnp.float32)
    left = (jax.nn.sigmoid(inner[:, H:2 * H]) * inner[:, :H]).astype(jnp.bfloat16)
    right = (jax.nn.sigmoid(inner[:, 3 * H:]) * inner[:, 2 * H:3 * H]).astype(jnp.bfloat16)
    gate = jax.nn.sigmoid(jnp.dot(flat, gate_weight, preferred_element_type=jnp.float32) + gate_bias.astype(jnp.float32))
    left_t = left.reshape(RESIDUES, RESIDUES, H).transpose(2, 0, 1).astype(jnp.float32)
    right_t = right.reshape(RESIDUES, RESIDUES, H).transpose(2, 0, 1).astype(jnp.float32)
    tri = jnp.einsum('hik,hjk->hij', left_t, right_t).transpose(1, 2, 0).astype(jnp.bfloat16)
    tri_normed = layer_norm(tri.astype(jnp.float32), out_gain, out_shift).astype(jnp.bfloat16)
    projected = jnp.dot(tri_normed.reshape(RESIDUES * RESIDUES, H), out_weight, preferred_element_type=jnp.float32)
    update = gate * (projected + out_bias.astype(jnp.float32))
    return update.reshape(RESIDUES, RESIDUES, C).astype(jnp.bfloat16)
```

```python
import functools

import jax
import jax.numpy as jnp
from jax import lax
from jax.experimental import pallas as pl
from jax.experimental.pallas import tpu as pltpu
from jax.sharding import PartitionSpec as P

MESH = pl.DeviceIdType.MESH
CHIPS = 128
ROWS = 16
BF16, F32 = jnp.bfloat16, jnp.float32
NT = (((1,), (1,)), ((), ()))


def sigmoid(x):
    return 0.5 * jnp.tanh(0.5 * x) + 0.5


def normalise(x, gain, shift):
    mean = jnp.sum(x, axis=0, keepdims=True) * (1.0 / 128)
    centred = x - mean
    variance = jnp.sum(centred * centred, axis=0, keepdims=True) * (1.0 / 128)
    return centred * lax.rsqrt(variance + 1e-05) * gain + shift


def twice(column):
    return jnp.concatenate([column, column], axis=1)


def kernel(
    pair, in_gain, in_shift, w_inner, inner_bias, gate_weight, gate_bias, out_gain, out_shift, out_weight, out_bias,
    out,
    cols, w_t, gw_t, ow_t, flat, normed, send1, recv1, left_m, right_m, acc, part_out, part_in, send2, recv2, gate,
    send1_sem, recv1_sem, part_send_sem, part_recv_sem, send2_sem, recv2_sem,
):
    row, col, ka = lax.axis_index("row"), lax.axis_index("col"), lax.axis_index("ka")
    core = lax.rem(ka, 2)
    x, z = (ka // 2) * 2 + row // 8, lax.rem(row, 8)
    me = (col * 2 + ka // 2) * ROWS + row

    def partner(step):
        tz = lax.rem(z + step % 8, 8)
        tx = lax.rem(x + (step // 8) % 4, 4)
        ty = lax.rem(col + step // 32, 4)
        trow = lax.rem(tx, 2) * 8 + tz
        return (ty * 2 + tx // 2) * ROWS + trow, (trow, ty, (tx // 2) * 2 + core)

    sibling = (row, col, (ka // 2) * 2 + 1 - core)

    barrier = pltpu.get_barrier_semaphore()

    def greet(step, _):
        pl.semaphore_signal(barrier, inc=1, device_id=partner(step)[1], device_id_type=MESH)
        return 0

    lax.fori_loop(1, CHIPS, greet, 0)
    pl.semaphore_signal(barrier, inc=1, device_id=sibling, device_id_type=MESH)

    rows = [in_gain[...], in_shift[...]]
    rows += [inner_bias[:, 128 * i : 128 * i + 128] for i in range(4)]
    rows += [gate_bias[...], out_gain[...], out_shift[...], out_bias[...]]
    for i, values in enumerate(rows):
        cols[i] = jnp.broadcast_to(values, (128, 128)).T
    w_t[...] = w_inner[...].astype(F32).T.astype(BF16)
    gw_t[...] = gate_weight[...].astype(F32).T.astype(BF16)
    ow_t[...] = out_weight[...].astype(F32).T.astype(BF16)

    def project(r, _):
        r0 = 2 * r
        block = jnp.concatenate([pair[r0], pair[r0 + 32], pair[r0 + 1], pair[r0 + 33]], axis=0)
        n = normalise(block.astype(F32).T, twice(cols[0]), twice(cols[1])).astype(BF16)
        normed[r] = n
        inner = jnp.dot(w_t[...], n, preferred_element_type=F32)
        left = sigmoid(inner[128:256] + twice(cols[3])) * (inner[:128] + twice(cols[2]))
        right = sigmoid(inner[384:] + twice(cols[5])) * (inner[256:384] + twice(cols[4]))
        for half in range(2):
            at = pl.multiple_of((r0 + half) * 256, 256)
            flat[pl.ds(at, 128), :] = left[:, half * 128 : half * 128 + 128]
            flat[pl.ds(at + 128, 128), :] = right[:, half * 128 : half * 128 + 128]
        return 0

    lax.fori_loop(0, 16, project, 0)
    pl.semaphore_wait(barrier, CHIPS)

    def channel(h):
        l = flat[pl.ds(h, 32, stride=256), :]
        r = flat[pl.ds(h + 128, 32, stride=256), :]
        return jnp.concatenate([l, r], axis=0).astype(BF16)

    def scatter(step, _):
        chip, device = partner(step)
        send1[chip] = channel(chip)
        pltpu.make_async_remote_copy(
            send1.at[chip], recv1.at[me], send1_sem, recv1_sem, device_id=device, device_id_type=MESH
        ).start()
        return 0

    lax.fori_loop(1, CHIPS, scatter, 0)
    recv1[me] = channel(me)

    def gates(r, _):
        g = jnp.dot(gw_t[...], normed[r], preferred_element_type=F32) + twice(cols[6])
        gate[r] = sigmoid(g)
        return 0

    lax.fori_loop(0, 16, gates, 0)

    others = pl.ds(0, CHIPS - 1)
    pltpu.make_async_copy(recv1.at[others], recv1.at[others], recv1_sem).wait()

    def assemble(b, _):
        at_l = pl.multiple_of(lax.rem(b, 4) * 256 + (b // 8) * 128 + (lax.rem(b, 8) // 4) * 64, 64)
        at_r = pl.multiple_of(lax.rem(b, 2) * 512 + (b // 2) * 64, 64)
        for p in range(4):
            one, two = recv1[2 * p * ROWS + b], recv1[(2 * p + 1) * ROWS + b]
            low = jnp.concatenate([one[:, :64], two[:, :64]], axis=1)
            high = jnp.concatenate([one[:, 64:], two[:, 64:]], axis=1)
            k = slice(p * 128, p * 128 + 128)
            left_m[pl.ds(at_l, 32), k] = low[:32]
            left_m[pl.ds(at_l + 32, 32), k] = high[:32]
            right_m[pl.ds(at_r, 32), k] = low[32:]
            right_m[pl.ds(at_r + 32, 32), k] = high[32:]
        return 0

    lax.fori_loop(0, ROWS, assemble, 0)

    def group(i):
        return lax.rem(lax.rem(z, 4) + i, 4)

    def part_copy(g):
        return pltpu.make_async_remote_copy(
            part_out.at[g], part_in.at[g], part_send_sem.at[g], part_recv_sem.at[g],
            device_id=sibling, device_id_type=MESH,
        )

    def block_product(g, half):
        lhs = left_m[pl.ds(pl.multiple_of(g * 256, 256), 256), :]
        rhs = right_m[pl.ds(pl.multiple_of(half * 512, 512), 512), :]
        return lax.dot_general(lhs, rhs, NT, preferred_element_type=F32)

    def multiply_other(i, _):
        g = group(i)
        part_out[g] = block_product(g, 1 - core).astype(BF16)
        part_copy(g).start()
        return 0

    def multiply_own(i, _):
        acc[group(i)] = block_product(group(i), core)
        return 0

    lax.fori_loop(0, 4, multiply_other, 0)
    lax.fori_loop(0, 4, multiply_own, 0)

    def give_back(i, _):
        g = group(i)
        part_copy(g).wait_recv()

        def per_row(j, _):
            at = pl.ds(pl.multiple_of(j * 64, 64), 64)
            trow = (j // 2) * 8 + lax.rem(j, 2) * 4 + g
            tri = (acc[g, at, :] + part_in[g, at, :].astype(F32)).astype(BF16)
            for kb in range(8):
                tile = jnp.concatenate([tri[:32, kb * 64 : kb * 64 + 64], tri[32:, kb * 64 : kb * 64 + 64]], axis=1)
                chip = kb * ROWS + trow

                @pl.when(chip == me)
                def _():
                    recv2[me] = tile

                @pl.when(chip != me)
                def _():
                    send2[chip] = tile
                    pltpu.make_async_remote_copy(
                        send2.at[chip], recv2.at[me], send2_sem, recv2_sem,
                        device_id=(trow, kb // 2, (kb % 2) * 2 + core), device_id_type=MESH,
                    ).start()

            return 0

        lax.fori_loop(0, 4, per_row, 0)
        return 0

    lax.fori_loop(0, 4, give_back, 0)
    pltpu.make_async_copy(recv2.at[others], recv2.at[others], recv2_sem).wait()

    def widen(h, _):
        flat[pl.ds(pl.multiple_of(h * 32, 32), 32), :] = recv2[h].astype(F32)
        return 0

    lax.fori_loop(0, CHIPS, widen, 0)

    def finish(r, _):
        r0 = 2 * r
        t = jnp.concatenate(
            [flat[pl.ds(r0, 128, stride=32), :], flat[pl.ds(r0 + 1, 128, stride=32), :]], axis=1
        )
        n = normalise(t, twice(cols[7]), twice(cols[8])).astype(BF16)
        projected = jnp.dot(ow_t[...], n, preferred_element_type=F32) + twice(cols[9])
        update = (gate[r] * projected).T.astype(BF16)
        out[r0] = update[:64]
        out[r0 + 32] = update[64:128]
        out[r0 + 1] = update[128:192]
        out[r0 + 33] = update[192:]
        return 0

    lax.fori_loop(0, 16, finish, 0)

    pltpu.make_async_copy(send1.at[others], send1.at[others], send1_sem).wait()
    pltpu.make_async_copy(send2.at[others], send2.at[others], send2_sem).wait()
    for g in range(4):
        part_copy(g).wait_send()


def on_device(pair, in_gain, in_shift, w_inner, inner_bias, gate_weight, gate_bias, out_gain, out_shift, out_weight, out_bias):
    vmem = pl.BlockSpec(memory_space=pltpu.VMEM)
    dma = pltpu.SemaphoreType.DMA
    as_row = lambda v: v.reshape(1, -1)
    return pl.pallas_call(
        kernel,
        out_shape=jax.ShapeDtypeStruct((64, 64, 128), BF16),
        in_specs=[vmem] * 11,
        out_specs=vmem,
        scratch_shapes=[
            pltpu.VMEM((10, 128, 128), F32),
            pltpu.VMEM((512, 128), BF16),
            pltpu.VMEM((128, 128), BF16),
            pltpu.VMEM((128, 128), BF16),
            pltpu.VMEM((32 * 256, 128), F32),
            pltpu.VMEM((16, 128, 256), BF16),
            pltpu.VMEM((CHIPS, 64, 128), BF16),
            pltpu.VMEM((CHIPS, 64, 128), BF16),
            pltpu.VMEM((1024, 512), BF16),
            pltpu.VMEM((1024, 512), BF16),
            pltpu.VMEM((4, 256, 512), F32),
            pltpu.VMEM((4, 256, 512), BF16),
            pltpu.VMEM((4, 256, 512), BF16),
            pltpu.VMEM((CHIPS, 32, 128), BF16),
            pltpu.VMEM((CHIPS, 32, 128), BF16),
            pltpu.VMEM((16, 128, 256), F32),
            dma, dma, dma((4,)), dma((4,)), dma, dma,
        ],
        compiler_params=pltpu.CompilerParams(
            collective_id=0, has_side_effects=True, vmem_limit_bytes=40 * 2**20
        ),
    )(
        pair, as_row(in_gain), as_row(in_shift), w_inner, as_row(inner_bias), gate_weight, as_row(gate_bias),
        as_row(out_gain), as_row(out_shift), out_weight, as_row(out_bias),
    )


def solution(mesh):
    placed = (P("row", ("col", "ka"), None),) + (P(),) * 10
    return jax.shard_map(
        on_device, mesh=mesh, in_specs=placed, out_specs=P("row", ("col", "ka"), None), check_vma=False
    )
```

```python
import functools

import jax
import jax.numpy as jnp
from jax import lax
from jax.experimental import pallas as pl
from jax.experimental.pallas import tpu as pltpu
from jax.sharding import PartitionSpec as P

MESH = pl.DeviceIdType.MESH
CHIPS = 128
ROWS = 16
BF16, F32 = jnp.bfloat16, jnp.float32
SMALL = [
    ((1, 128), F32), ((1, 128), F32), ((128, 512), BF16), ((1, 512), F32), ((128, 128), BF16),
    ((1, 128), F32), ((1, 128), F32), ((1, 128), F32), ((128, 128), BF16), ((1, 128), F32),
]
NT = (((1,), (1,)), ((), ()))


def sigmoid(x):
    return 0.5 * jnp.tanh(0.5 * x) + 0.5


def normalise(x, gain, shift):
    mean = jnp.sum(x, axis=0, keepdims=True) * (1.0 / 128)
    centred = x - mean
    variance = jnp.sum(centred * centred, axis=0, keepdims=True) * (1.0 / 128)
    return centred * lax.rsqrt(variance + 1e-05) * gain + shift


def twice(column):
    return jnp.concatenate([column, column], axis=1)


def kernel(
    pair_hbm, *refs
):
    small_hbm, out_hbm, refs = refs[:10], refs[10], refs[11:]
    small, refs = refs[:10], refs[10:]
    in_gain, in_shift, w_inner, inner_bias, gate_weight, gate_bias, out_gain, out_shift, out_weight, out_bias = small
    (
    pair, out, small_sem, pair_sem, out_sem, plane_sem, all_sem,
    cols, w_t, gw_t, ow_t, flat, normed, send1, recv1, left_m, right_m, acc, part_out, part_in, send2, recv2, gate,
    send1_sem, recv1_sem, part_send_sem, part_recv_sem, send2_sem, recv2_sem,
    ) = refs
    small_copies = [pltpu.make_async_copy(a, b, small_sem.at[i]) for i, (a, b) in enumerate(zip(small_hbm, small))]

    def quarter(src, dst, sem, c):
        return [
            pltpu.make_async_copy(src.at[pl.ds(8 * c + h, 8)], dst.at[pl.ds(8 * c + h, 8)], sem.at[c, h // 32])
            for h in (0, 32)
        ]

    for copy in small_copies + [copy for c in range(4) for copy in quarter(pair_hbm, pair, pair_sem, c)]:
        copy.start()
    row, col, ka = lax.axis_index("row"), lax.axis_index("col"), lax.axis_index("ka")
    core = lax.rem(ka, 2)
    x, z = (ka // 2) * 2 + row // 8, lax.rem(row, 8)
    me = (col * 2 + ka // 2) * ROWS + row

    def partner(step):
        tz = lax.rem(z + step % 8, 8)
        tx = lax.rem(x + (step // 8) % 4, 4)
        ty = lax.rem(col + step // 32, 4)
        trow = lax.rem(tx, 2) * 8 + tz
        return (ty * 2 + tx // 2) * ROWS + trow, (trow, ty, (tx // 2) * 2 + core)

    sibling = (row, col, (ka // 2) * 2 + 1 - core)

    barrier = pltpu.get_barrier_semaphore()

    def line(axis, d):
        tz = lax.rem(z + d, 8) if axis == "z" else z
        tx = lax.rem(x + d, 4) if axis == "x" else x
        ty = lax.rem(col + d, 4) if axis == "y" else col
        return (lax.rem(tx, 2) * 8 + tz, ty, (tx // 2) * 2 + core)

    def greet(sem, axis, count):
        for d in range(1, count):
            pl.semaphore_signal(sem, inc=1, device_id=line(axis, d), device_id_type=MESH)

    greet(barrier, "z", 8)
    greet(barrier, "x", 4)
    greet(barrier, "y", 4)
    pl.semaphore_signal(barrier, inc=1, device_id=sibling, device_id_type=MESH)

    for copy in small_copies:
        copy.wait()
    rows = [in_gain[...], in_shift[...]]
    rows += [inner_bias[:, 128 * i : 128 * i + 128] for i in range(4)]
    rows += [gate_bias[...], out_gain[...], out_shift[...], out_bias[...]]
    for i, values in enumerate(rows):
        cols[i] = jnp.broadcast_to(values, (128, 128)).T
    w_t[...] = w_inner[...].astype(F32).T.astype(BF16)
    gw_t[...] = gate_weight[...].astype(F32).T.astype(BF16)
    ow_t[...] = out_weight[...].astype(F32).T.astype(BF16)

    def project(r, _):
        r0 = 2 * r
        block = jnp.concatenate([pair[r0], pair[r0 + 32], pair[r0 + 1], pair[r0 + 33]], axis=0)
        n = normalise(block.astype(F32).T, twice(cols[0]), twice(cols[1])).astype(BF16)
        normed[r] = n
        inner = jnp.dot(w_t[...], n, preferred_element_type=F32)
        left = sigmoid(inner[128:256] + twice(cols[3])) * (inner[:128] + twice(cols[2]))
        right = sigmoid(inner[384:] + twice(cols[5])) * (inner[256:384] + twice(cols[4]))
        for half in range(2):
            at = pl.multiple_of((r0 + half) * 256, 256)
            flat[pl.ds(at, 128), :] = left[:, half * 128 : half * 128 + 128]
            flat[pl.ds(at + 128, 128), :] = right[:, half * 128 : half * 128 + 128]
        return 0

    def project_quarter(c):
        for copy in quarter(pair_hbm, pair, pair_sem, c):
            copy.wait()
        lax.fori_loop(4 * c, 4 * c + 4, project, 0, unroll=4)

    project_quarter(0)
    project_quarter(1)
    pl.semaphore_wait(barrier, 14)
    greet(plane_sem, "x", 4)
    project_quarter(2)
    pl.semaphore_wait(plane_sem, 3)
    greet(all_sem, "y", 4)
    project_quarter(3)
    pl.semaphore_wait(all_sem, 3)

    def channel(h):
        l = flat[pl.ds(h, 32, stride=256), :]
        r = flat[pl.ds(h + 128, 32, stride=256), :]
        return jnp.concatenate([l, r], axis=0).astype(BF16)

    def scatter(step, _):
        chip, device = partner(step)
        send1[chip] = channel(chip)
        pltpu.make_async_remote_copy(
            send1.at[chip], recv1.at[me], send1_sem, recv1_sem, device_id=device, device_id_type=MESH
        ).start()
        return 0

    lax.fori_loop(1, CHIPS, scatter, 0)
    recv1[me] = channel(me)

    def gates(r, _):
        g = jnp.dot(gw_t[...], normed[r], preferred_element_type=F32) + twice(cols[6])
        gate[r] = sigmoid(g)
        return 0

    lax.fori_loop(0, 16, gates, 0, unroll=2)

    others = pl.ds(0, CHIPS - 1)
    pltpu.make_async_copy(recv1.at[others], recv1.at[others], recv1_sem).wait()

    def assemble(b, _):
        at_l = pl.multiple_of(lax.rem(b, 4) * 256 + (b // 8) * 128 + (lax.rem(b, 8) // 4) * 64, 64)
        at_r = pl.multiple_of(lax.rem(b, 2) * 512 + (b // 2) * 64, 64)
        for p in range(4):
            one, two = recv1[2 * p * ROWS + b], recv1[(2 * p + 1) * ROWS + b]
            low = jnp.concatenate([one[:, :64], two[:, :64]], axis=1)
            high = jnp.concatenate([one[:, 64:], two[:, 64:]], axis=1)
            k = slice(p * 128, p * 128 + 128)
            left_m[pl.ds(at_l, 32), k] = low[:32]
            left_m[pl.ds(at_l + 32, 32), k] = high[:32]
            right_m[pl.ds(at_r, 32), k] = low[32:]
            right_m[pl.ds(at_r + 32, 32), k] = high[32:]
        return 0

    lax.fori_loop(0, ROWS, assemble, 0)

    def group(i):
        return lax.rem(lax.rem(z, 4) + i, 4)

    def part_copy(g):
        return pltpu.make_async_remote_copy(
            part_out.at[g], part_in.at[g], part_send_sem.at[g], part_recv_sem.at[g],
            device_id=sibling, device_id_type=MESH,
        )

    def block_product(g, half):
        lhs = left_m[pl.ds(pl.multiple_of(g * 256, 256), 256), :]
        rhs = right_m[pl.ds(pl.multiple_of(half * 512, 512), 512), :]
        return lax.dot_general(lhs, rhs, NT, preferred_element_type=F32)

    def multiply_other(i, _):
        g = group(i)
        part_out[g] = block_product(g, 1 - core).astype(BF16)
        part_copy(g).start()
        return 0

    def multiply_own(i, _):
        acc[group(i)] = block_product(group(i), core)
        return 0

    lax.fori_loop(0, 4, multiply_other, 0)
    lax.fori_loop(0, 4, multiply_own, 0)

    def give_back(i, _):
        g = group(i)
        part_copy(g).wait_recv()

        def per_row(j, _):
            at = pl.ds(pl.multiple_of(j * 64, 64), 64)
            trow = (j // 2) * 8 + lax.rem(j, 2) * 4 + g
            tri = (acc[g, at, :] + part_in[g, at, :].astype(F32)).astype(BF16)
            for kb in range(8):
                tile = jnp.concatenate([tri[:32, kb * 64 : kb * 64 + 64], tri[32:, kb * 64 : kb * 64 + 64]], axis=1)
                chip = kb * ROWS + trow

                @pl.when(chip == me)
                def _():
                    recv2[me] = tile

                @pl.when(chip != me)
                def _():
                    send2[chip] = tile
                    pltpu.make_async_remote_copy(
                        send2.at[chip], recv2.at[me], send2_sem, recv2_sem,
                        device_id=(trow, kb // 2, (kb % 2) * 2 + core), device_id_type=MESH,
                    ).start()

            return 0

        lax.fori_loop(0, 4, per_row, 0)
        return 0

    lax.fori_loop(0, 4, give_back, 0)
    pltpu.make_async_copy(recv2.at[others], recv2.at[others], recv2_sem).wait()

    def widen(h, _):
        flat[pl.ds(pl.multiple_of(h * 32, 32), 32), :] = recv2[h].astype(F32)
        return 0

    lax.fori_loop(0, CHIPS, widen, 0)

    def finish(r, _):
        r0 = 2 * r
        t = jnp.concatenate(
            [flat[pl.ds(r0, 128, stride=32), :], flat[pl.ds(r0 + 1, 128, stride=32), :]], axis=1
        )
        n = normalise(t, twice(cols[7]), twice(cols[8])).astype(BF16)
        projected = jnp.dot(ow_t[...], n, preferred_element_type=F32) + twice(cols[9])
        update = (gate[r] * projected).T.astype(BF16)
        out[r0] = update[:64]
        out[r0 + 32] = update[64:128]
        out[r0 + 1] = update[128:192]
        out[r0 + 33] = update[192:]
        return 0

    for c in range(4):
        lax.fori_loop(4 * c, 4 * c + 4, finish, 0, unroll=4)
        for copy in quarter(out, out_hbm, out_sem, c):
            copy.start()

    pltpu.make_async_copy(send1.at[others], send1.at[others], send1_sem).wait()
    pltpu.make_async_copy(send2.at[others], send2.at[others], send2_sem).wait()
    for g in range(4):
        part_copy(g).wait_send()
    for c in range(4):
        for copy in quarter(out, out_hbm, out_sem, c):
            copy.wait()


def on_device(pair, in_gain, in_shift, w_inner, inner_bias, gate_weight, gate_bias, out_gain, out_shift, out_weight, out_bias):
    anywhere = pl.BlockSpec(memory_space=pl.ANY)
    dma = pltpu.SemaphoreType.DMA
    as_row = lambda v: v.reshape(1, -1)
    return pl.pallas_call(
        kernel,
        out_shape=jax.ShapeDtypeStruct((64, 64, 128), BF16),
        in_specs=[anywhere] * 11,
        out_specs=anywhere,
        scratch_shapes=[
            *(pltpu.VMEM(shape, dtype) for shape, dtype in SMALL),
            pltpu.VMEM((64, 64, 128), BF16),
            pltpu.VMEM((64, 64, 128), BF16),
            dma((10,)), dma((4, 2)), dma((4, 2)), pltpu.SemaphoreType.REGULAR, pltpu.SemaphoreType.REGULAR,
            pltpu.VMEM((10, 128, 128), F32),
            pltpu.VMEM((512, 128), BF16),
            pltpu.VMEM((128, 128), BF16),
            pltpu.VMEM((128, 128), BF16),
            pltpu.VMEM((32 * 256, 128), F32),
            pltpu.VMEM((16, 128, 256), BF16),
            pltpu.VMEM((CHIPS, 64, 128), BF16),
            pltpu.VMEM((CHIPS, 64, 128), BF16),
            pltpu.VMEM((1024, 512), BF16),
            pltpu.VMEM((1024, 512), BF16),
            pltpu.VMEM((4, 256, 512), F32),
            pltpu.VMEM((4, 256, 512), BF16),
            pltpu.VMEM((4, 256, 512), BF16),
            pltpu.VMEM((CHIPS, 32, 128), BF16),
            pltpu.VMEM((CHIPS, 32, 128), BF16),
            pltpu.VMEM((16, 128, 256), F32),
            dma, dma, dma((4,)), dma((4,)), dma, dma,
        ],
        compiler_params=pltpu.CompilerParams(
            collective_id=0, has_side_effects=True, vmem_limit_bytes=56 * 2**20
        ),
    )(
        pair, as_row(in_gain), as_row(in_shift), w_inner, as_row(inner_bias), gate_weight, as_row(gate_bias),
        as_row(out_gain), as_row(out_shift), out_weight, as_row(out_bias),
    )


def solution(mesh):
    placed = (P("row", ("col", "ka"), None),) + (P(),) * 10
    return jax.shard_map(
        on_device, mesh=mesh, in_specs=placed, out_specs=P("row", ("col", "ka"), None), check_vma=False
    )
```

```python
import functools

import jax
import jax.numpy as jnp
from jax import lax
from jax.experimental import pallas as pl
from jax.experimental.pallas import tpu as pltpu
from jax.sharding import PartitionSpec as P

MESH = pl.DeviceIdType.MESH
CHIPS = 128
ROWS = 16
BF16, F32 = jnp.bfloat16, jnp.float32
SMALL = [
    ((1, 128), F32), ((1, 128), F32), ((128, 512), BF16), ((1, 512), F32), ((128, 128), BF16),
    ((1, 128), F32), ((1, 128), F32), ((1, 128), F32), ((128, 128), BF16), ((1, 128), F32),
]
NT = (((1,), (1,)), ((), ()))


def sigmoid(x):
    return 0.5 * jnp.tanh(0.5 * x) + 0.5


def normalise(x, gain, shift):
    mean = jnp.sum(x, axis=0, keepdims=True) * (1.0 / 128)
    centred = x - mean
    variance = jnp.sum(centred * centred, axis=0, keepdims=True) * (1.0 / 128)
    return centred * lax.rsqrt(variance + 1e-05) * gain + shift


def twice(column):
    return jnp.concatenate([column, column], axis=1)


def kernel(
    pair_hbm, *refs
):
    small_hbm, out_hbm, refs = refs[:10], refs[10], refs[11:]
    small, refs = refs[:10], refs[10:]
    in_gain, in_shift, w_inner, inner_bias, gate_weight, gate_bias, out_gain, out_shift, out_weight, out_bias = small
    (
    pair, out, small_sem, pair_sem, out_sem, plane_sem, all_sem,
    cols, w_t, gw_t, ow_t, flat, normed, send_l, recv_l, send_r, recv_r, left_m, right_m, acc, part_out, part_in,
    send2, recv2, gate,
    send_l_sem, recv_l_sem, send_r_sem, recv_r_sem, part_send_sem, part_recv_sem, send2_sem, recv2_sem,
    ) = refs
    small_copies = [pltpu.make_async_copy(a, b, small_sem.at[i]) for i, (a, b) in enumerate(zip(small_hbm, small))]

    def quarter(src, dst, sem, c):
        return [
            pltpu.make_async_copy(src.at[pl.ds(8 * c + h, 8)], dst.at[pl.ds(8 * c + h, 8)], sem.at[c, h // 32])
            for h in (0, 32)
        ]

    for copy in small_copies + [copy for c in range(4) for copy in quarter(pair_hbm, pair, pair_sem, c)]:
        copy.start()
    row, col, ka = lax.axis_index("row"), lax.axis_index("col"), lax.axis_index("ka")
    core = lax.rem(ka, 2)
    x_hi, x_lo = lax.div(ka, 2), lax.div(row, 8)
    x, z = x_hi * 2 + x_lo, lax.rem(row, 8)
    me = (col * 2 + x_hi) * ROWS + row

    z_at = [lax.rem(z + d, 8) for d in range(8)]

    def partners(dx, dy, dzs):
        tx, ty = lax.rem(x + dx, 4), lax.rem(col + dy, 4)
        hi = lax.div(tx, 2)
        lo = (tx - 2 * hi) * 8
        base, ka_to = (ty * 2 + hi) * ROWS + lo, hi * 2 + core
        return [(base + z_at[d], (lo + z_at[d], ty, ka_to)) for d in dzs]

    sibling = (row, col, x_hi * 2 + 1 - core)

    barrier = pltpu.get_barrier_semaphore()

    def line(axis, d):
        tz = lax.rem(z + d, 8) if axis == "z" else z
        tx = lax.rem(x + d, 4) if axis == "x" else x
        ty = lax.rem(col + d, 4) if axis == "y" else col
        return (lax.rem(tx, 2) * 8 + tz, ty, (tx // 2) * 2 + core)

    def greet(sem, axis, count):
        for d in range(1, count):
            pl.semaphore_signal(sem, inc=1, device_id=line(axis, d), device_id_type=MESH)

    greet(barrier, "z", 8)
    greet(barrier, "x", 4)
    greet(barrier, "y", 4)
    pl.semaphore_signal(barrier, inc=1, device_id=sibling, device_id_type=MESH)

    for copy in small_copies:
        copy.wait()
    rows = [in_gain[...], in_shift[...]]
    rows += [inner_bias[:, 128 * i : 128 * i + 128] for i in range(4)]
    rows += [gate_bias[...], out_gain[...], out_shift[...], out_bias[...]]
    for i, values in enumerate(rows):
        cols[i] = jnp.broadcast_to(values, (128, 128)).T
    w_t[...] = w_inner[...].astype(F32).T.astype(BF16)
    gw_t[...] = gate_weight[...].astype(F32).T.astype(BF16)
    ow_t[...] = out_weight[...].astype(F32).T.astype(BF16)

    def project(r, _):
        r0 = 2 * r
        block = jnp.concatenate([pair[r0], pair[r0 + 32], pair[r0 + 1], pair[r0 + 33]], axis=0)
        n = normalise(block.astype(F32).T, twice(cols[0]), twice(cols[1])).astype(BF16)
        normed[r] = n
        inner = jnp.dot(w_t[...], n, preferred_element_type=F32)
        left = sigmoid(inner[128:256] + twice(cols[3])) * (inner[:128] + twice(cols[2]))
        right = sigmoid(inner[384:] + twice(cols[5])) * (inner[256:384] + twice(cols[4]))
        for half in range(2):
            at = pl.multiple_of((r0 + half) * 256, 256)
            flat[pl.ds(at, 128), :] = left[:, half * 128 : half * 128 + 128]
            flat[pl.ds(at + 128, 128), :] = right[:, half * 128 : half * 128 + 128]
        return 0

    def project_quarter(c):
        for copy in quarter(pair_hbm, pair, pair_sem, c):
            copy.wait()
        lax.fori_loop(4 * c, 4 * c + 4, project, 0, unroll=4)

    def channel(first, h):
        return flat[pl.ds(first + h, 32, stride=256), :].astype(BF16)

    def send_left(dx, dy, dzs=(0, 4, 1, 7, 2, 6, 3, 5)):
        for chip, device in partners(dx, dy, dzs):
            send_l[chip] = channel(0, chip)
            pltpu.make_async_remote_copy(
                send_l.at[chip], recv_l.at[me], send_l_sem, recv_l_sem, device_id=device, device_id_type=MESH
            ).start()
        return 0

    def z_steps(g):
        return (g, 8 - g) if g else (0, 4)

    def send_right(g):
        def send(dy, first):
            for dx in range(4):
                for chip, device in partners(dx, dy, z_steps(g)[1 if first and dx == 0 else 0 :]):
                    send_r[chip] = channel(128, chip)
                    pltpu.make_async_remote_copy(
                        send_r.at[chip], recv_r.at[me], send_r_sem, recv_r_sem.at[g],
                        device_id=device, device_id_type=MESH,
                    ).start()
            return 0

        if g == 0:
            send(0, True)
        lax.fori_loop(0 if g else 1, 4, lambda dy, _: send(dy, False), 0)

    project_quarter(0)
    project_quarter(1)
    pl.semaphore_wait(barrier, 14)
    greet(plane_sem, "x", 4)
    project_quarter(2)
    project_quarter(3)
    send_left(0, 0, (4, 1, 7, 2, 6, 3, 5))
    pl.semaphore_wait(plane_sem, 3)
    greet(all_sem, "y", 4)
    lax.fori_loop(1, 4, lambda dx, _: send_left(dx, 0), 0)
    pl.semaphore_wait(all_sem, 3)
    lax.fori_loop(1, 4, lambda dy, _: lax.fori_loop(0, 4, lambda dx, _: send_left(dx, dy), 0), 0)
    for g in range(4):
        send_right(g)
    recv_l[me] = channel(0, me)
    recv_r[me] = channel(128, me)

    def gates(r, _):
        g = jnp.dot(gw_t[...], normed[r], preferred_element_type=F32) + twice(cols[6])
        gate[r] = sigmoid(g)
        return 0

    lax.fori_loop(0, 16, gates, 0, unroll=2)

    others = pl.ds(0, CHIPS - 1)
    pltpu.make_async_copy(recv_l.at[others], recv_l.at[others], recv_l_sem).wait()

    def assemble(src, b, dst, at):
        for p in range(4):
            one, two = src[2 * p * ROWS + b], src[(2 * p + 1) * ROWS + b]
            k = slice(p * 128, p * 128 + 128)
            dst[pl.ds(at, 32), k] = jnp.concatenate([one[:, :64], two[:, :64]], axis=1)
            dst[pl.ds(at + 32, 32), k] = jnp.concatenate([one[:, 64:], two[:, 64:]], axis=1)

    def assemble_left(b, _):
        assemble(recv_l, b, left_m, pl.multiple_of(b * 64, 64))
        return 0

    lax.fori_loop(0, ROWS, assemble_left, 0)

    def part_copy(slot, m):
        return pltpu.make_async_remote_copy(
            part_out.at[slot, m], part_in.at[slot, m], part_send_sem.at[slot, m], part_recv_sem.at[slot, m],
            device_id=sibling, device_id_type=MESH,
        )

    def multiply(g):
        one, two = z_steps(g)
        slot = g // 2
        some = pl.ds(0, 32 if g else 31)
        pltpu.make_async_copy(recv_r.at[some], recv_r.at[some], recv_r_sem.at[g]).wait()
        zs = [z_at[one], z_at[two]]
        kbs = [(n // 2) * 4 + lax.div(zs[n % 2], 2) for n in range(4)]
        homes = [(lax.div(kb, 2), lax.rem(kb, 2) * 2 + core) for kb in kbs]
        for n in range(4):
            assemble(recv_r, (n // 2) * 8 + zs[n % 2], right_m, n * 64)

        def product(m):
            lhs = left_m[pl.ds(pl.multiple_of(m * 256, 256), 256), :]
            return lax.dot_general(lhs, right_m[...], NT, preferred_element_type=F32)

        own = lax.rem(z + g, 2) == core

        @pl.when(jnp.logical_not(own))
        def _():
            def for_sibling(m, _):
                part_out[slot, m] = product(m).astype(BF16)
                part_copy(slot, m).start()
                return 0

            lax.fori_loop(0, 4, for_sibling, 0)

        @pl.when(own)
        def _():
            def for_us(m, _):
                acc[m] = product(m)
                return 0

            lax.fori_loop(0, 4, for_us, 0)

            def tiles(m, _):
                part_copy(slot, m).wait_recv()
                tri = (acc[m] + part_in[slot, m].astype(F32)).astype(BF16)
                for b in range(4):
                    for n in range(4):
                        low = tri[b * 64 : b * 64 + 32, n * 64 : n * 64 + 64]
                        high = tri[b * 64 + 32 : b * 64 + 64, n * 64 : n * 64 + 64]
                        send2[kbs[n] * ROWS + m * 4 + b] = jnp.concatenate([low, high], axis=1)
                return 0

            lax.fori_loop(0, 4, tiles, 0)

            def give_back(a, half, here):
                part = slice(half * 16, half * 16 + 16)
                tz = lax.rem(z + 3 * a, 8)
                for n in range(4):
                    for lo in (0, 8):
                        chip, device = kbs[n] * ROWS + lo + tz, (lo + tz, *homes[n])
                        copy = pltpu.make_async_remote_copy(
                            send2.at[chip, part], recv2.at[me, part], send2_sem, recv2_sem.at[half],
                            device_id=device, device_id_type=MESH,
                        )
                        if not here:
                            copy.start()
                            continue

                        @pl.when(chip == me)
                        def _():
                            recv2[me, part] = send2[me, part]

                        @pl.when(chip != me)
                        def _():
                            copy.start()

                return 0

            for half in range(2):
                lax.fori_loop(1, 8, lambda a, _: give_back(a, half, False), 0)
                give_back(0, half, True)

    for g in range(4):
        multiply(g)

    def widen(half):
        def one(h, _):
            at = pl.multiple_of(h * 32 + half * 16, 16)
            flat[pl.ds(at, 16), :] = recv2[h, pl.ds(half * 16, 16)].astype(F32)
            return 0

        return one

    def finish(r, _):
        r0 = 2 * r
        t = jnp.concatenate(
            [flat[pl.ds(r0, 128, stride=32), :], flat[pl.ds(r0 + 1, 128, stride=32), :]], axis=1
        )
        n = normalise(t, twice(cols[7]), twice(cols[8])).astype(BF16)
        projected = jnp.dot(ow_t[...], n, preferred_element_type=F32) + twice(cols[9])
        update = (gate[r] * projected).T.astype(BF16)
        out[r0] = update[:64]
        out[r0 + 32] = update[64:128]
        out[r0 + 1] = update[128:192]
        out[r0 + 33] = update[192:]
        return 0

    for half in range(2):
        rows_in = recv2.at[others, pl.ds(half * 16, 16)]
        pltpu.make_async_copy(rows_in, rows_in, recv2_sem.at[half]).wait()
        lax.fori_loop(0, CHIPS, widen(half), 0, unroll=4)
        for c in (2 * half, 2 * half + 1):
            lax.fori_loop(4 * c, 4 * c + 4, finish, 0, unroll=4)
            for copy in quarter(out, out_hbm, out_sem, c):
                copy.start()

    pltpu.make_async_copy(send_l.at[others], send_l.at[others], send_l_sem).wait()
    pltpu.make_async_copy(send_r.at[others], send_r.at[others], send_r_sem).wait()
    pltpu.make_async_copy(send2.at[others], send2.at[others], send2_sem).wait()
    for g in range(4):

        @pl.when(lax.rem(z + g, 2) != core)
        def _():
            for m in range(4):
                part_copy(g // 2, m).wait_send()

    for c in range(4):
        for copy in quarter(out, out_hbm, out_sem, c):
            copy.wait()


def on_device(pair, in_gain, in_shift, w_inner, inner_bias, gate_weight, gate_bias, out_gain, out_shift, out_weight, out_bias):
    anywhere = pl.BlockSpec(memory_space=pl.ANY)
    dma = pltpu.SemaphoreType.DMA
    as_row = lambda v: v.reshape(1, -1)
    return pl.pallas_call(
        kernel,
        out_shape=jax.ShapeDtypeStruct((64, 64, 128), BF16),
        in_specs=[anywhere] * 11,
        out_specs=anywhere,
        scratch_shapes=[
            *(pltpu.VMEM(shape, dtype) for shape, dtype in SMALL),
            pltpu.VMEM((64, 64, 128), BF16),
            pltpu.VMEM((64, 64, 128), BF16),
            dma((10,)), dma((4, 2)), dma((4, 2)), pltpu.SemaphoreType.REGULAR, pltpu.SemaphoreType.REGULAR,
            pltpu.VMEM((10, 128, 128), F32),
            pltpu.VMEM((512, 128), BF16),
            pltpu.VMEM((128, 128), BF16),
            pltpu.VMEM((128, 128), BF16),
            pltpu.VMEM((32 * 256, 128), F32),
            pltpu.VMEM((16, 128, 256), BF16),
            *[pltpu.VMEM((CHIPS, 32, 128), BF16)] * 4,
            pltpu.VMEM((1024, 512), BF16),
            pltpu.VMEM((256, 512), BF16),
            pltpu.VMEM((4, 256, 256), F32),
            *[pltpu.VMEM((2, 4, 256, 256), BF16)] * 2,
            *[pltpu.VMEM((CHIPS, 32, 128), BF16)] * 2,
            pltpu.VMEM((16, 128, 256), F32),
            dma, dma, dma, dma((4,)), dma((2, 4)), dma((2, 4)), dma, dma((2,)),
        ],
        compiler_params=pltpu.CompilerParams(
            collective_id=0, has_side_effects=True, vmem_limit_bytes=56 * 2**20
        ),
    )(
        pair, as_row(in_gain), as_row(in_shift), w_inner, as_row(inner_bias), gate_weight, as_row(gate_bias),
        as_row(out_gain), as_row(out_shift), out_weight, as_row(out_bias),
    )


def solution(mesh):
    placed = (P("row", ("col", "ka"), None),) + (P(),) * 10
    return jax.shard_map(
        on_device, mesh=mesh, in_specs=placed, out_specs=P("row", ("col", "ka"), None), check_vma=False
    )
```

```python
import functools

import jax
import jax.numpy as jnp
from jax import lax
from jax.experimental import pallas as pl
from jax.experimental.pallas import tpu as pltpu
from jax.sharding import PartitionSpec as P

MESH = pl.DeviceIdType.MESH
CHIPS = 128
ROWS = 16
BF16, F32 = jnp.bfloat16, jnp.float32
SMALL = [
    ((1, 128), F32), ((1, 128), F32), ((128, 512), BF16), ((1, 512), F32), ((128, 128), BF16),
    ((1, 128), F32), ((1, 128), F32), ((1, 128), F32), ((128, 128), BF16), ((1, 128), F32),
]
NT = (((1,), (1,)), ((), ()))


def sigmoid(x):
    return 0.5 * jnp.tanh(0.5 * x) + 0.5


def normalise(x, gain, shift):
    mean = jnp.sum(x, axis=0, keepdims=True) * (1.0 / 128)
    centred = x - mean
    variance = jnp.sum(centred * centred, axis=0, keepdims=True) * (1.0 / 128)
    return centred * lax.rsqrt(variance + 1e-05) * gain + shift


def twice(column):
    return jnp.concatenate([column, column], axis=1)


def kernel(
    pair_hbm, *refs
):
    small_hbm, out_hbm, refs = refs[:10], refs[10], refs[11:]
    small, refs = refs[:10], refs[10:]
    in_gain, in_shift, w_inner, inner_bias, gate_weight, gate_bias, out_gain, out_shift, out_weight, out_bias = small
    (
    pair, out, small_sem, pair_sem, out_sem, plane_sem, all_sem,
    cols, w_t, gw_t, ow_t, flat, normed, send_l, recv_l, send_r, recv_r, passed, left_m, right_m, acc, part_out, part_in,
    send2, recv2, gate,
    send_l_sem, recv_l_sem, send_r_sem, recv_r_sem, pass_send_sem, pass_recv_sem, part_send_sem, part_recv_sem, send2_sem, recv2_sem,
    ) = refs
    small_copies = [pltpu.make_async_copy(a, b, small_sem.at[i]) for i, (a, b) in enumerate(zip(small_hbm, small))]

    def quarter(src, dst, sem, c):
        return [
            pltpu.make_async_copy(src.at[pl.ds(8 * c + h, 8)], dst.at[pl.ds(8 * c + h, 8)], sem.at[c, h // 32])
            for h in (0, 32)
        ]

    row, col, ka = lax.axis_index("row"), lax.axis_index("col"), lax.axis_index("ka")
    core = lax.rem(ka, 2)
    x_hi, x_lo = lax.div(ka, 2), lax.div(row, 8)
    x, z = x_hi * 2 + x_lo, lax.rem(row, 8)
    me = (col * 2 + x_hi) * ROWS + row

    z_at = [lax.rem(z + d, 8) for d in range(8)]

    mine = (me, me - z + z_at[7])
    place = x_lo * 8 + col * 2 + x_hi

    def partners(dx, dy, ds):
        tx, ty = lax.rem(x + dx, 4), lax.rem(col + dy, 4)
        hi = lax.div(tx, 2)
        lo = (tx - 2 * hi) * 8
        base, ka_to = (ty * 2 + hi) * ROWS + lo, hi * 2 + core
        return [
            (base + z_at[d], (lo + z_at[d if d < 4 else (d + 1) % 8], ty, ka_to), (d if d < 4 else 11 - d) * 16 + place)
            for d in ds
        ]

    sibling = (row, col, x_hi * 2 + 1 - core)

    barrier = pltpu.get_barrier_semaphore()

    def line(axis, d):
        tz = lax.rem(z + d, 8) if axis == "z" else z
        tx = lax.rem(x + d, 4) if axis == "x" else x
        ty = lax.rem(col + d, 4) if axis == "y" else col
        return (lax.rem(tx, 2) * 8 + tz, ty, (tx // 2) * 2 + core)

    def greet(sem, axis, count):
        for d in range(1, count):
            pl.semaphore_signal(sem, inc=1, device_id=line(axis, d), device_id_type=MESH)

    greet(barrier, "z", 8)
    greet(barrier, "x", 4)
    greet(barrier, "y", 4)
    pl.semaphore_signal(barrier, inc=1, device_id=sibling, device_id_type=MESH)

    for copy in small_copies + [copy for c in range(4) for copy in quarter(pair_hbm, pair, pair_sem, c)]:
        copy.start()
    rows = [(in_gain, 0), (in_shift, 0), *((inner_bias, 128 * i) for i in range(4))]
    rows += [(gate_bias, 0), (out_gain, 0), (out_shift, 0), (out_bias, 0)]

    def columns(which):
        for i in which:
            ref, at = rows[i]
            cols[i] = jnp.broadcast_to(ref[:, at : at + 128], (128, 128)).T

    def turned(weight):
        return weight.astype(F32).T.astype(BF16)

    def branch(n, first):
        inner = jnp.dot(w_t[first * 128 : first * 128 + 256], n, preferred_element_type=F32)
        return sigmoid(inner[128:] + twice(cols[first + 3])) * (inner[:128] + twice(cols[first + 2]))

    def keep(values, r, first):
        for half in range(2):
            at = pl.multiple_of((2 * r + half) * 256 + first, 128)
            flat[pl.ds(at, 128), :] = values[:, half * 128 : half * 128 + 128]

    def project_left(r, _):
        r0 = 2 * r
        block = jnp.concatenate([pair[r0], pair[r0 + 32], pair[r0 + 1], pair[r0 + 33]], axis=0)
        n = normalise(block.astype(F32).T, twice(cols[0]), twice(cols[1])).astype(BF16)
        normed[r] = n
        keep(branch(n, 0), r, 0)
        return 0

    def project_right(r, _):
        keep(branch(normed[r], 2), r, 128)
        return 0

    def left_quarter(c):
        for copy in quarter(pair_hbm, pair, pair_sem, c):
            copy.wait()
        lax.fori_loop(4 * c, 4 * c + 4, project_left, 0, unroll=4)

    def channel(first, h):
        return flat[pl.ds(first + h, 32, stride=256), :].astype(BF16)

    def send_left(dx, dy, ds=(0, 7, 1, 6, 2, 5, 3, 4)):
        for chip, device, slot in partners(dx, dy, ds):
            send_l[chip] = channel(0, chip)
            pltpu.make_async_remote_copy(
                send_l.at[chip], recv_l.at[slot], send_l_sem, recv_l_sem, device_id=device, device_id_type=MESH
            ).start()
        return 0

    def send_right(j):
        def send(dy, dxs):
            for dx in dxs:
                for chip, device, slot in partners(dx, dy, (j, 7 - j)):
                    send_r[chip] = channel(128, chip)
                    pltpu.make_async_remote_copy(
                        send_r.at[chip], recv_r.at[slot], send_r_sem, recv_r_sem.at[j],
                        device_id=device, device_id_type=MESH,
                    ).start()
            return 0

        if j == 0:
            send(0, (1, 2, 3))
        lax.fori_loop(0 if j else 1, 4, lambda dy, _: send(dy, range(4)), 0)

    for i in (0, 1, 2, 3):
        small_copies[i].wait()
    columns(range(4))
    w_t[:256] = turned(w_inner[:, :256])
    left_quarter(0)
    left_quarter(1)
    pl.semaphore_wait(barrier, 14)
    greet(plane_sem, "x", 4)
    left_quarter(2)
    left_quarter(3)
    send_left(0, 0, (1, 6, 2, 5, 3, 4))
    pl.semaphore_wait(plane_sem, 3)
    greet(all_sem, "y", 4)
    lax.fori_loop(1, 4, lambda dx, _: send_left(dx, 0), 0)
    for copy in small_copies[4:]:
        copy.wait()
    columns(range(4, 10))
    w_t[256:] = turned(w_inner[:, 256:])
    gw_t[...] = turned(gate_weight[...])
    ow_t[...] = turned(out_weight[...])
    lax.fori_loop(0, 16, project_right, 0, unroll=4)
    pl.semaphore_wait(all_sem, 3)
    lax.fori_loop(1, 4, lambda dy, _: lax.fori_loop(0, 4, lambda dx, _: send_left(dx, dy), 0), 0)
    for role in range(2):
        recv_l[role * 64 + place] = channel(0, mine[role])
        recv_r[role * 64 + place] = channel(128, mine[role])
    for j in range(4):
        send_right(j)

    def gates(r, _):
        g = jnp.dot(gw_t[...], normed[r], preferred_element_type=F32) + twice(cols[6])
        gate[r] = sigmoid(g)
        return 0

    lax.fori_loop(0, 16, gates, 0, unroll=2)

    others = pl.ds(0, CHIPS - 2)
    pltpu.make_async_copy(recv_l.at[others], recv_l.at[others], recv_l_sem).wait()

    def assemble(src, b, dst, at):
        for p in range(4):
            one, two = src[b * 8 + 2 * p], src[b * 8 + 2 * p + 1]
            k = slice(p * 128, p * 128 + 128)
            dst[pl.ds(at, 32), k] = jnp.concatenate([one[:, :64], two[:, :64]], axis=1)
            dst[pl.ds(at + 32, 32), k] = jnp.concatenate([one[:, 64:], two[:, 64:]], axis=1)

    def assemble_left(b, _):
        assemble(recv_l, b, left_m, pl.multiple_of(b * 64, 64))
        return 0

    lax.fori_loop(0, ROWS, assemble_left, 0)

    def pass_copy(role, j):
        return pltpu.make_async_remote_copy(
            recv_r.at[pl.ds((role * 4 + j) * 16, 16)], passed.at[pl.ds(((1 - role) * 4 + j) * 16, 16)],
            pass_send_sem.at[role, j], pass_recv_sem.at[1 - role, j],
            device_id=line("z", 7 if role else 1), device_id_type=MESH,
        )

    def passed_here(role, j):
        ref = passed.at[pl.ds((role * 4 + j) * 16, 16)]
        return pltpu.make_async_copy(ref, ref, pass_recv_sem.at[role, j])

    def part_copy(t, m):
        columns = pl.ds(0, 256 if 0 < t < 4 else 128)
        return pltpu.make_async_remote_copy(
            part_out.at[t // 2, m, :, columns], part_in.at[t // 2, m, :, columns],
            part_send_sem.at[t // 2, m], part_recv_sem.at[t // 2, m], device_id=sibling, device_id_type=MESH,
        )

    def multiply(t):
        if t < 4:
            some = pl.ds(0, 32 if t else 30)
            pltpu.make_async_copy(recv_r.at[some], recv_r.at[some], recv_r_sem.at[t]).wait()
            for role in range(2):
                pass_copy(role, t).start()
        if t > 0:
            for role in range(2):
                passed_here(role, t - 1).wait()
        planes = [z_at[8 - t], z_at[t]] if 0 < t < 4 else [z_at[t]]
        blocks = 2 * len(planes)
        width = 64 * blocks
        kbs = [(n % 2) * 4 + lax.div(planes[n // 2], 2) for n in range(blocks)]
        homes = [(lax.div(kb, 2), lax.rem(kb, 2) * 2 + core) for kb in kbs]
        for role in range(2):
            for n in range(blocks):
                direct = t == 0 or (t < 4 and n // 2 == role)
                src, j = (recv_r, t) if direct else (passed, t - 1)
                assemble(src, (role * 4 + j) * 2 + n % 2, right_m, role * 256 + n * 64)

        def product(m):
            lhs = left_m[pl.ds(pl.multiple_of(m * 256, 256), 256), :]
            rhs = right_m[pl.ds(pl.multiple_of(lax.div(m, 2) * 256, 256), width), :]
            return lax.dot_general(lhs, rhs, NT, preferred_element_type=F32)

        own = lax.rem(z + t, 2) == core

        @pl.when(jnp.logical_not(own))
        def _():
            def for_sibling(m, _):
                part_out[t // 2, m, :, :width] = product(m).astype(BF16)
                part_copy(t, m).start()
                return 0

            lax.fori_loop(0, 4, for_sibling, 0)

        @pl.when(own)
        def _():
            def for_us(m, _):
                acc[m, :, :width] = product(m)
                return 0

            lax.fori_loop(0, 4, for_us, 0)

            def tiles(m, _):
                part_copy(t, m).wait_recv()
                tri = (acc[m, :, :width] + part_in[t // 2, m, :, :width].astype(F32)).astype(BF16)
                for b in range(4):
                    for n in range(blocks):
                        low = tri[b * 64 : b * 64 + 32, n * 64 : n * 64 + 64]
                        high = tri[b * 64 + 32 : b * 64 + 64, n * 64 : n * 64 + 64]
                        send2[(m * 4 + b) * 8 + kbs[n]] = jnp.concatenate([low, high], axis=1)
                return 0

            lax.fori_loop(0, 4, tiles, 0)

            def give_back(j, half, here):
                part = slice(half * 16, half * 16 + 16)
                for n in range(blocks):
                    for role, tz in ((0, lax.rem(z + 8 - j, 8)), (1, lax.rem(z + j, 8))):
                        for lo in range(2):
                            tile = ((role * 4 + j) * 2 + lo) * 8 + kbs[n]
                            copy = pltpu.make_async_remote_copy(
                                send2.at[tile, part], recv2.at[mine[role], part], send2_sem, recv2_sem.at[half],
                                device_id=(lo * 8 + tz, *homes[n]), device_id_type=MESH,
                            )
                            if not here:
                                copy.start()
                                continue
                            ours = (kbs[n] * ROWS + lo * 8 + z) == me

                            @pl.when(ours)
                            def _():
                                recv2[mine[role], part] = send2[tile, part]

                            @pl.when(jnp.logical_not(ours))
                            def _():
                                copy.start()

                return 0

            for half in range(2):
                lax.fori_loop(1, 4, lambda j, _: give_back(j, half, False), 0)
                give_back(0, half, True)

    for t in range(5):
        multiply(t)

    def widen(half):
        def one(h, _):
            at = pl.multiple_of(h * 32 + half * 16, 16)
            flat[pl.ds(at, 16), :] = recv2[h, pl.ds(half * 16, 16)].astype(F32)
            return 0

        return one

    def finish(r, _):
        r0 = 2 * r
        t = jnp.concatenate(
            [flat[pl.ds(r0, 128, stride=32), :], flat[pl.ds(r0 + 1, 128, stride=32), :]], axis=1
        )
        n = normalise(t, twice(cols[7]), twice(cols[8])).astype(BF16)
        projected = jnp.dot(ow_t[...], n, preferred_element_type=F32) + twice(cols[9])
        update = (gate[r] * projected).T.astype(BF16)
        out[r0] = update[:64]
        out[r0 + 32] = update[64:128]
        out[r0 + 1] = update[128:192]
        out[r0 + 33] = update[192:]
        return 0

    for half in range(2):
        rows_in = recv2.at[others, pl.ds(half * 16, 16)]
        pltpu.make_async_copy(rows_in, rows_in, recv2_sem.at[half]).wait()
        lax.fori_loop(0, CHIPS, widen(half), 0, unroll=4)
        for c in (2 * half, 2 * half + 1):
            lax.fori_loop(4 * c, 4 * c + 4, finish, 0, unroll=4)
            for copy in quarter(out, out_hbm, out_sem, c):
                copy.start()

    pltpu.make_async_copy(send_l.at[others], send_l.at[others], send_l_sem).wait()
    pltpu.make_async_copy(send_r.at[others], send_r.at[others], send_r_sem).wait()
    pltpu.make_async_copy(send2.at[others], send2.at[others], send2_sem).wait()
    for role in range(2):
        for j in range(4):
            pass_copy(role, j).wait_send()
    for t in range(5):

        @pl.when(lax.rem(z + t, 2) != core)
        def _():
            for m in range(4):
                part_copy(t, m).wait_send()

    for c in range(4):
        for copy in quarter(out, out_hbm, out_sem, c):
            copy.wait()


def on_device(pair, in_gain, in_shift, w_inner, inner_bias, gate_weight, gate_bias, out_gain, out_shift, out_weight, out_bias):
    anywhere = pl.BlockSpec(memory_space=pl.ANY)
    dma = pltpu.SemaphoreType.DMA
    as_row = lambda v: v.reshape(1, -1)
    return pl.pallas_call(
        kernel,
        out_shape=jax.ShapeDtypeStruct((64, 64, 128), BF16),
        in_specs=[anywhere] * 11,
        out_specs=anywhere,
        scratch_shapes=[
            *(pltpu.VMEM(shape, dtype) for shape, dtype in SMALL),
            pltpu.VMEM((64, 64, 128), BF16),
            pltpu.VMEM((64, 64, 128), BF16),
            dma((10,)), dma((4, 2)), dma((4, 2)), pltpu.SemaphoreType.REGULAR, pltpu.SemaphoreType.REGULAR,
            pltpu.VMEM((10, 128, 128), F32),
            pltpu.VMEM((512, 128), BF16),
            pltpu.VMEM((128, 128), BF16),
            pltpu.VMEM((128, 128), BF16),
            pltpu.VMEM((32 * 256, 128), F32),
            pltpu.VMEM((16, 128, 256), BF16),
            *[pltpu.VMEM((CHIPS, 32, 128), BF16)] * 5,
            pltpu.VMEM((1024, 512), BF16),
            pltpu.VMEM((512, 512), BF16),
            pltpu.VMEM((4, 256, 256), F32),
            *[pltpu.VMEM((3, 4, 256, 256), BF16)] * 2,
            *[pltpu.VMEM((CHIPS, 32, 128), BF16)] * 2,
            pltpu.VMEM((16, 128, 256), F32),
            dma, dma, dma, dma((4,)), dma((2, 4)), dma((2, 4)), dma((3, 4)), dma((3, 4)), dma, dma((2,)),
        ],
        compiler_params=pltpu.CompilerParams(
            collective_id=0, has_side_effects=True, vmem_limit_bytes=56 * 2**20
        ),
    )(
        pair, as_row(in_gain), as_row(in_shift), w_inner, as_row(inner_bias), gate_weight, as_row(gate_bias),
        as_row(out_gain), as_row(out_shift), out_weight, as_row(out_bias),
    )


def solution(mesh):
    placed = (P("row", ("col", "ka"), None),) + (P(),) * 10
    return jax.shard_map(
        on_device, mesh=mesh, in_specs=placed, out_specs=P("row", ("col", "ka"), None), check_vma=False
    )
```

```python
import functools

import jax
import jax.numpy as jnp
from jax import lax
from jax.experimental import pallas as pl
from jax.experimental.pallas import tpu as pltpu
from jax.sharding import PartitionSpec as P

MESH = pl.DeviceIdType.MESH
CHIPS = 128
ROWS = 16
BF16, F32 = jnp.bfloat16, jnp.float32
SMALL = [
    ((1, 128), F32), ((1, 128), F32), ((128, 512), BF16), ((1, 512), F32), ((128, 128), BF16),
    ((1, 128), F32), ((1, 128), F32), ((1, 128), F32), ((128, 128), BF16), ((1, 128), F32),
]
NT = (((1,), (1,)), ((), ()))


def sigmoid(x):
    return 0.5 * jnp.tanh(0.5 * x) + 0.5


def normalise(x, gain, shift):
    mean = jnp.sum(x, axis=0, keepdims=True) * (1.0 / 128)
    centred = x - mean
    variance = jnp.sum(centred * centred, axis=0, keepdims=True) * (1.0 / 128)
    return centred * lax.rsqrt(variance + 1e-05) * gain + shift


def twice(column):
    return jnp.concatenate([column, column], axis=1)


def kernel(
    pair_hbm, *refs
):
    small_hbm, out_hbm, refs = refs[:10], refs[10], refs[11:]
    small, refs = refs[:10], refs[10:]
    in_gain, in_shift, w_inner, inner_bias, gate_weight, gate_bias, out_gain, out_shift, out_weight, out_bias = small
    (
    pair, out, small_sem, pair_sem, out_sem, plane_sem, all_sem,
    cols, w_t, gw_t, ow_t, flat, normed, send_l, recv_l, send_r, recv_r, passed, left_m, right_m, acc, part_out, part_in,
    send2, recv2, gate,
    send_l_sem, recv_l_sem, send_r_sem, recv_r_sem, pass_send_sem, pass_recv_sem, part_send_sem, part_recv_sem, send2_sem, recv2_sem,
    ) = refs
    small_copies = [pltpu.make_async_copy(a, b, small_sem.at[i]) for i, (a, b) in enumerate(zip(small_hbm, small))]

    def quarter(src, dst, sem, c):
        return [
            pltpu.make_async_copy(src.at[pl.ds(8 * c + h, 8)], dst.at[pl.ds(8 * c + h, 8)], sem.at[c, h // 32])
            for h in (0, 32)
        ]

    row, col, ka = lax.axis_index("row"), lax.axis_index("col"), lax.axis_index("ka")
    core = lax.rem(ka, 2)
    x_hi, x_lo = lax.div(ka, 2), lax.div(row, 8)
    x, z = x_hi * 2 + x_lo, lax.rem(row, 8)
    me = (col * 2 + x_hi) * ROWS + row

    z_at = [lax.rem(z + d, 8) for d in range(8)]

    mine = (me, me - z + z_at[7])
    place = x_lo * 8 + col * 2 + x_hi

    def partners(dx, dy, ds):
        tx, ty = lax.rem(x + dx, 4), lax.rem(col + dy, 4)
        hi = lax.div(tx, 2)
        lo = (tx - 2 * hi) * 8
        base, ka_to = (ty * 2 + hi) * ROWS + lo, hi * 2 + core
        return [
            (base + z_at[d], (lo + z_at[d if d < 4 else (d + 1) % 8], ty, ka_to), (d if d < 4 else 11 - d) * 16 + place)
            for d in ds
        ]

    sibling = (row, col, x_hi * 2 + 1 - core)

    barrier = pltpu.get_barrier_semaphore()

    def line(axis, d):
        tz = lax.rem(z + d, 8) if axis == "z" else z
        tx = lax.rem(x + d, 4) if axis == "x" else x
        ty = lax.rem(col + d, 4) if axis == "y" else col
        return (lax.rem(tx, 2) * 8 + tz, ty, (tx // 2) * 2 + core)

    def greet(sem, axis, count):
        for d in range(1, count):
            pl.semaphore_signal(sem, inc=1, device_id=line(axis, d), device_id_type=MESH)

    greet(barrier, "z", 8)
    greet(barrier, "x", 4)
    greet(barrier, "y", 4)
    pl.semaphore_signal(barrier, inc=1, device_id=sibling, device_id_type=MESH)

    for copy in small_copies + [copy for c in range(4) for copy in quarter(pair_hbm, pair, pair_sem, c)]:
        copy.start()
    rows = [(in_gain, 0), (in_shift, 0), *((inner_bias, 128 * i) for i in range(4))]
    rows += [(gate_bias, 0), (out_gain, 0), (out_shift, 0), (out_bias, 0)]

    def columns(which):
        for i in which:
            ref, at = rows[i]
            cols[i] = jnp.broadcast_to(ref[:, at : at + 128], (128, 128)).T

    def turned(weight):
        return weight.astype(F32).T.astype(BF16)

    def branch(n, first):
        inner = jnp.dot(w_t[first * 128 : first * 128 + 256], n, preferred_element_type=F32)
        return sigmoid(inner[128:] + twice(cols[first + 3])) * (inner[:128] + twice(cols[first + 2]))

    def keep(values, r, first):
        for half in range(2):
            at = pl.multiple_of((2 * r + half) * 256 + first, 128)
            flat[pl.ds(at, 128), :] = values[:, half * 128 : half * 128 + 128]

    def project_right(r, _):
        r0 = 2 * r
        block = jnp.concatenate([pair[r0], pair[r0 + 32], pair[r0 + 1], pair[r0 + 33]], axis=0)
        n = normalise(block.astype(F32).T, twice(cols[0]), twice(cols[1])).astype(BF16)
        normed[r] = n
        keep(branch(n, 2), r, 128)
        return 0

    def project_left(r, _):
        keep(branch(normed[r], 0), r, 0)
        return 0

    def right_quarter(c):
        for copy in quarter(pair_hbm, pair, pair_sem, c):
            copy.wait()
        lax.fori_loop(4 * c, 4 * c + 4, project_right, 0, unroll=4)

    def channel(first, h):
        return flat[pl.ds(first + h, 32, stride=256), :].astype(BF16)

    def send_right(dx, dy, ds=(0, 7, 1, 6, 2, 5, 3, 4)):
        for chip, device, slot in partners(dx, dy, ds):
            send_r[chip] = channel(128, chip)
            pltpu.make_async_remote_copy(
                send_r.at[chip], recv_r.at[slot], send_r_sem, recv_r_sem, device_id=device, device_id_type=MESH
            ).start()
        return 0

    def send_left(j):
        def send(dy, dxs):
            for dx in dxs:
                for chip, device, slot in partners(dx, dy, (j, 7 - j)):
                    send_l[chip] = channel(0, chip)
                    pltpu.make_async_remote_copy(
                        send_l.at[chip], recv_l.at[slot], send_l_sem, recv_l_sem.at[j],
                        device_id=device, device_id_type=MESH,
                    ).start()
            return 0

        if j == 0:
            send(0, (1, 2, 3))
        lax.fori_loop(0 if j else 1, 4, lambda dy, _: send(dy, range(4)), 0)

    for i in (0, 1, 2, 3):
        small_copies[i].wait()
    columns((0, 1, 4, 5))
    w_t[256:] = turned(w_inner[:, 256:])
    right_quarter(0)
    right_quarter(1)
    pl.semaphore_wait(barrier, 14)
    greet(plane_sem, "x", 4)
    right_quarter(2)
    right_quarter(3)
    send_right(0, 0, (1, 6, 2, 5, 3, 4))
    pl.semaphore_wait(plane_sem, 3)
    greet(all_sem, "y", 4)
    lax.fori_loop(1, 4, lambda dx, _: send_right(dx, 0), 0)
    for copy in small_copies[4:]:
        copy.wait()
    columns((2, 3, 6, 7, 8, 9))
    w_t[:256] = turned(w_inner[:, :256])
    gw_t[...] = turned(gate_weight[...])
    ow_t[...] = turned(out_weight[...])
    lax.fori_loop(0, 16, project_left, 0, unroll=4)
    pl.semaphore_wait(all_sem, 3)
    lax.fori_loop(1, 4, lambda dy, _: lax.fori_loop(0, 4, lambda dx, _: send_right(dx, dy), 0), 0)
    for role in range(2):
        recv_l[role * 64 + place] = channel(0, mine[role])
        recv_r[role * 64 + place] = channel(128, mine[role])
    send_left(3)

    def pass_copy(role):
        return pltpu.make_async_remote_copy(
            recv_r.at[pl.ds(role * 64, 64)], passed.at[pl.ds((1 - role) * 64, 64)],
            pass_send_sem.at[role], pass_recv_sem.at[1 - role],
            device_id=line("z", 7 if role else 1), device_id_type=MESH,
        )

    others = pl.ds(0, CHIPS - 2)
    pltpu.make_async_copy(recv_r.at[others], recv_r.at[others], recv_r_sem).wait()
    for role in range(2):
        pass_copy(role).start()
    for j in (2, 1, 0):
        send_left(j)

    def gates(r, _):
        g = jnp.dot(gw_t[...], normed[r], preferred_element_type=F32) + twice(cols[6])
        gate[r] = sigmoid(g)
        return 0

    lax.fori_loop(0, 16, gates, 0, unroll=2)

    def assemble(src, b, dst, at):
        for p in range(4):
            one, two = src[b * 8 + 2 * p], src[b * 8 + 2 * p + 1]
            k = slice(p * 128, p * 128 + 128)
            dst[pl.ds(at, 32), k] = jnp.concatenate([one[:, :64], two[:, :64]], axis=1)
            dst[pl.ds(at + 32, 32), k] = jnp.concatenate([one[:, 64:], two[:, 64:]], axis=1)

    def assemble_right(src, role, j, plane):
        for lo in range(2):
            at = role * 1024 + lax.rem(plane, 2) * 512 + (lo * 4 + lax.div(plane, 2)) * 64
            assemble(src, (role * 4 + j) * 2 + lo, right_m, pl.multiple_of(at, 64))

    def direct(j, _):
        assemble_right(recv_r, 0, j, lax.rem(z + 8 - j, 8))
        assemble_right(recv_r, 1, j, lax.rem(z + j, 8))
        return 0

    def indirect(j, _):
        assemble_right(passed, 0, j, lax.rem(z + 1 + j, 8))
        assemble_right(passed, 1, j, lax.rem(z + 7 - j, 8))
        return 0

    lax.fori_loop(0, 4, direct, 0)
    for role in range(2):
        ref = passed.at[pl.ds(role * 64, 64)]
        pltpu.make_async_copy(ref, ref, pass_recv_sem.at[role]).wait()
    lax.fori_loop(0, 4, indirect, 0)

    def part_copy(t, role):
        return pltpu.make_async_remote_copy(
            part_out.at[t, role], part_in.at[t, role], part_send_sem.at[t, role], part_recv_sem.at[t, role],
            device_id=sibling, device_id_type=MESH,
        )

    def product(role, half):
        rhs = right_m[pl.ds(pl.multiple_of(role * 1024 + half * 512, 512), 512), :]
        return lax.dot_general(left_m[role * 128 : role * 128 + 128], rhs, NT, preferred_element_type=F32)

    def multiply(t):
        some = pl.ds(0, 32 if t else 30)
        pltpu.make_async_copy(recv_l.at[some], recv_l.at[some], recv_l_sem.at[t]).wait()
        for role in range(2):
            for lo in range(2):
                assemble(recv_l, (role * 4 + t) * 2 + lo, left_m, role * 128 + lo * 64)
        for role in range(2):
            part_out[t, role] = product(role, 1 - core).astype(BF16)
            part_copy(t, role).start()
        for role in range(2):
            acc[role] = product(role, core)
        for role in range(2):
            part_copy(t, role).wait_recv()
            tri = (acc[role] + part_in[t, role].astype(F32)).astype(BF16)
            for lo in range(2):
                for kb in range(8):
                    low = tri[lo * 64 : lo * 64 + 32, kb * 64 : kb * 64 + 64]
                    high = tri[lo * 64 + 32 : lo * 64 + 64, kb * 64 : kb * 64 + 64]
                    send2[((role * 4 + t) * 2 + lo) * 8 + kb] = jnp.concatenate([low, high], axis=1)

        def give_back(step, half):
            part = slice(half * 16, half * 16 + 16)
            kb = lax.rem(col * 2 + x_hi + step, 8)
            y_to = lax.div(kb, 2)
            ka_to = lax.rem(kb, 2) * 2 + core
            for role in range(2):
                for lo in range(2):
                    tile = ((role * 4 + t) * 2 + lo) * 8 + kb
                    row_to = lo * 8 + z_at[t if role else (8 - t) % 8]
                    copy = pltpu.make_async_remote_copy(
                        send2.at[tile, part], recv2.at[mine[role], part], send2_sem, recv2_sem.at[half],
                        device_id=(row_to, y_to, ka_to), device_id_type=MESH,
                    )
                    if t:
                        copy.start()
                        continue
                    ours = kb * ROWS + row_to == me

                    @pl.when(ours)
                    def _():
                        recv2[mine[role], part] = send2[tile, part]

                    @pl.when(jnp.logical_not(ours))
                    def _():
                        copy.start()

            return 0

        for half in range(2):
            lax.fori_loop(0, 8, lambda step, _: give_back(step, half), 0)

    for t in (3, 2, 1, 0):
        multiply(t)

    def widen(half):
        def one(h, _):
            at = pl.multiple_of(h * 32 + half * 16, 16)
            flat[pl.ds(at, 16), :] = recv2[h, pl.ds(half * 16, 16)].astype(F32)
            return 0

        return one

    def finish(r, _):
        r0 = 2 * r
        t = jnp.concatenate(
            [flat[pl.ds(r0, 128, stride=32), :], flat[pl.ds(r0 + 1, 128, stride=32), :]], axis=1
        )
        n = normalise(t, twice(cols[7]), twice(cols[8])).astype(BF16)
        projected = jnp.dot(ow_t[...], n, preferred_element_type=F32) + twice(cols[9])
        update = (gate[r] * projected).T.astype(BF16)
        out[r0] = update[:64]
        out[r0 + 32] = update[64:128]
        out[r0 + 1] = update[128:192]
        out[r0 + 33] = update[192:]
        return 0

    for half in range(2):
        rows_in = recv2.at[others, pl.ds(half * 16, 16)]
        pltpu.make_async_copy(rows_in, rows_in, recv2_sem.at[half]).wait()
        lax.fori_loop(0, CHIPS, widen(half), 0, unroll=4)
        for c in (2 * half, 2 * half + 1):
            lax.fori_loop(4 * c, 4 * c + 4, finish, 0, unroll=4)
            for copy in quarter(out, out_hbm, out_sem, c):
                copy.start()

    pltpu.make_async_copy(send_l.at[others], send_l.at[others], send_l_sem).wait()
    pltpu.make_async_copy(send_r.at[others], send_r.at[others], send_r_sem).wait()
    pltpu.make_async_copy(send2.at[others], send2.at[others], send2_sem).wait()
    for role in range(2):
        pass_copy(role).wait_send()
        for t in range(4):
            part_copy(t, role).wait_send()
    for c in range(4):
        for copy in quarter(out, out_hbm, out_sem, c):
            copy.wait()


def on_device(pair, in_gain, in_shift, w_inner, inner_bias, gate_weight, gate_bias, out_gain, out_shift, out_weight, out_bias):
    anywhere = pl.BlockSpec(memory_space=pl.ANY)
    dma = pltpu.SemaphoreType.DMA
    as_row = lambda v: v.reshape(1, -1)
    return pl.pallas_call(
        kernel,
        out_shape=jax.ShapeDtypeStruct((64, 64, 128), BF16),
        in_specs=[anywhere] * 11,
        out_specs=anywhere,
        scratch_shapes=[
            *(pltpu.VMEM(shape, dtype) for shape, dtype in SMALL),
            pltpu.VMEM((64, 64, 128), BF16),
            pltpu.VMEM((64, 64, 128), BF16),
            dma((10,)), dma((4, 2)), dma((4, 2)), pltpu.SemaphoreType.REGULAR, pltpu.SemaphoreType.REGULAR,
            pltpu.VMEM((10, 128, 128), F32),
            pltpu.VMEM((512, 128), BF16),
            pltpu.VMEM((128, 128), BF16),
            pltpu.VMEM((128, 128), BF16),
            pltpu.VMEM((32 * 256, 128), F32),
            pltpu.VMEM((16, 128, 256), BF16),
            *[pltpu.VMEM((CHIPS, 32, 128), BF16)] * 5,
            pltpu.VMEM((256, 512), BF16),
            pltpu.VMEM((2048, 512), BF16),
            pltpu.VMEM((2, 128, 512), F32),
            *[pltpu.VMEM((4, 2, 128, 512), BF16)] * 2,
            *[pltpu.VMEM((CHIPS, 32, 128), BF16)] * 2,
            pltpu.VMEM((16, 128, 256), F32),
            dma, dma((4,)), dma, dma, dma((2,)), dma((2,)), dma((4, 2)), dma((4, 2)), dma, dma((2,)),
        ],
        compiler_params=pltpu.CompilerParams(
            collective_id=0, has_side_effects=True, vmem_limit_bytes=56 * 2**20
        ),
    )(
        pair, as_row(in_gain), as_row(in_shift), w_inner, as_row(inner_bias), gate_weight, as_row(gate_bias),
        as_row(out_gain), as_row(out_shift), out_weight, as_row(out_bias),
    )


def solution(mesh):
    placed = (P("row", ("col", "ka"), None),) + (P(),) * 10
    return jax.shard_map(
        on_device, mesh=mesh, in_specs=placed, out_specs=P("row", ("col", "ka"), None), check_vma=False
    )
```

```python
import functools

import jax
import jax.numpy as jnp
from jax import lax
from jax.experimental import pallas as pl
from jax.experimental.pallas import tpu as pltpu
from jax.sharding import PartitionSpec as P

MESH = pl.DeviceIdType.MESH
CHIPS = 128
ROWS = 16
BF16, F32 = jnp.bfloat16, jnp.float32
SMALL = [
    ((1, 128), F32), ((1, 128), F32), ((128, 512), BF16), ((1, 512), F32), ((128, 128), BF16),
    ((1, 128), F32), ((1, 128), F32), ((1, 128), F32), ((128, 128), BF16), ((1, 128), F32),
]
NT = (((1,), (1,)), ((), ()))


def sigmoid(x):
    return 0.5 * jnp.tanh(0.5 * x) + 0.5


def normalise(x, gain, shift):
    mean = jnp.sum(x, axis=0, keepdims=True) * (1.0 / 128)
    centred = x - mean
    variance = jnp.sum(centred * centred, axis=0, keepdims=True) * (1.0 / 128)
    return centred * lax.rsqrt(variance + 1e-05) * gain + shift


def twice(column):
    return jnp.concatenate([column, column], axis=1)


def kernel(
    pair_hbm, *refs
):
    small_hbm, out_hbm, refs = refs[:10], refs[10], refs[11:]
    small, refs = refs[:10], refs[10:]
    in_gain, in_shift, w_inner, inner_bias, gate_weight, gate_bias, out_gain, out_shift, out_weight, out_bias = small
    (
    pair, out, small_sem, pair_sem, out_sem, plane_sem, all_sem,
    cols, w_t, gw_t, ow_t, flat, normed, send_l, recv_l, send_r, recv_r, passed, left_m, right_m, acc, part_out, part_in,
    send2, recv2, gate,
    send_l_sem, recv_l_sem, send_r_sem, recv_r_sem, pass_send_sem, pass_recv_sem, part_send_sem, part_recv_sem, send2_sem, recv2_sem,
    ) = refs
    small_copies = [pltpu.make_async_copy(a, b, small_sem.at[i]) for i, (a, b) in enumerate(zip(small_hbm, small))]

    def quarter(src, dst, sem, c):
        return [
            pltpu.make_async_copy(src.at[pl.ds(8 * c + h, 8)], dst.at[pl.ds(8 * c + h, 8)], sem.at[c, h // 32])
            for h in (0, 32)
        ]

    row, col, ka = lax.axis_index("row"), lax.axis_index("col"), lax.axis_index("ka")
    core = lax.rem(ka, 2)
    x_hi, x_lo = lax.div(ka, 2), lax.div(row, 8)
    x, z = x_hi * 2 + x_lo, lax.rem(row, 8)
    me = (col * 2 + x_hi) * ROWS + row

    z_at = [lax.rem(z + d, 8) for d in range(8)]

    mine = (me, me - z + z_at[7])
    place = x_lo * 8 + col * 2 + x_hi

    def partners(dx, dy, ds):
        tx, ty = lax.rem(x + dx, 4), lax.rem(col + dy, 4)
        hi = lax.div(tx, 2)
        lo = (tx - 2 * hi) * 8
        base, ka_to = (ty * 2 + hi) * ROWS + lo, hi * 2 + core
        return [
            (base + z_at[d], (lo + z_at[d if d < 4 else (d + 1) % 8], ty, ka_to), (d if d < 4 else 11 - d) * 16 + place)
            for d in ds
        ]

    sibling = (row, col, x_hi * 2 + 1 - core)

    barrier = pltpu.get_barrier_semaphore()

    def line(axis, d):
        tz = lax.rem(z + d, 8) if axis == "z" else z
        tx = lax.rem(x + d, 4) if axis == "x" else x
        ty = lax.rem(col + d, 4) if axis == "y" else col
        return (lax.rem(tx, 2) * 8 + tz, ty, (tx // 2) * 2 + core)

    def greet(sem, axis, count):
        for d in range(1, count):
            pl.semaphore_signal(sem, inc=1, device_id=line(axis, d), device_id_type=MESH)

    greet(barrier, "z", 8)
    greet(barrier, "x", 4)
    greet(barrier, "y", 4)
    pl.semaphore_signal(barrier, inc=1, device_id=sibling, device_id_type=MESH)

    for copy in small_copies + [copy for c in range(4) for copy in quarter(pair_hbm, pair, pair_sem, c)]:
        copy.start()
    rows = [(in_gain, 0), (in_shift, 0), *((inner_bias, 128 * i) for i in range(4))]
    rows += [(gate_bias, 0), (out_gain, 0), (out_shift, 0), (out_bias, 0)]

    def columns(which):
        for i in which:
            ref, at = rows[i]
            cols[i] = jnp.broadcast_to(ref[:, at : at + 128], (128, 128)).T

    def turned(weight):
        return weight.astype(F32).T.astype(BF16)

    def branch(n, first):
        inner = jnp.dot(w_t[first * 128 : first * 128 + 256], n, preferred_element_type=F32)
        return sigmoid(inner[128:] + twice(cols[first + 3])) * (inner[:128] + twice(cols[first + 2]))

    def keep(values, r, first):
        for half in range(2):
            at = pl.multiple_of((2 * r + half) * 256 + first, 128)
            flat[pl.ds(at, 128), :] = values[:, half * 128 : half * 128 + 128]

    def project_right(r, _):
        r0 = 2 * r
        block = jnp.concatenate([pair[r0], pair[r0 + 32], pair[r0 + 1], pair[r0 + 33]], axis=0)
        n = normalise(block.astype(F32).T, twice(cols[0]), twice(cols[1])).astype(BF16)
        normed[r] = n
        keep(branch(n, 2), r, 128)
        return 0

    def project_left(r, _):
        keep(branch(normed[r], 0), r, 0)
        return 0

    def right_quarter(c):
        for copy in quarter(pair_hbm, pair, pair_sem, c):
            copy.wait()
        lax.fori_loop(4 * c, 4 * c + 4, project_right, 0, unroll=4)

    def channel(first, h):
        return flat[pl.ds(first + h, 32, stride=256), :].astype(BF16)

    def send_right(dx, dy, ds=(0, 7, 1, 6, 2, 5, 3, 4)):
        for chip, device, slot in partners(dx, dy, ds):
            send_r[chip] = channel(128, chip)
            pltpu.make_async_remote_copy(
                send_r.at[chip], recv_r.at[slot], send_r_sem, recv_r_sem, device_id=device, device_id_type=MESH
            ).start()
        return 0

    def send_left(j):
        def send(dy, dxs):
            for dx in dxs:
                for chip, device, slot in partners(dx, dy, (j, 7 - j)):
                    send_l[chip] = channel(0, chip)
                    pltpu.make_async_remote_copy(
                        send_l.at[chip], recv_l.at[slot], send_l_sem, recv_l_sem.at[j],
                        device_id=device, device_id_type=MESH,
                    ).start()
            return 0

        if j == 0:
            send(0, (1, 2, 3))
        lax.fori_loop(0 if j else 1, 4, lambda dy, _: send(dy, range(4)), 0)

    for i in (0, 1, 2, 3):
        small_copies[i].wait()
    columns((0, 1, 4, 5))
    w_t[256:] = turned(w_inner[:, 256:])
    right_quarter(0)
    right_quarter(1)
    pl.semaphore_wait(barrier, 14)
    greet(plane_sem, "x", 4)
    right_quarter(2)
    right_quarter(3)
    send_right(0, 0, (1, 6, 2, 5, 3, 4))
    pl.semaphore_wait(plane_sem, 3)
    greet(all_sem, "y", 4)
    lax.fori_loop(1, 4, lambda dx, _: send_right(dx, 0), 0)
    for copy in small_copies[4:]:
        copy.wait()
    columns((2, 3, 6, 7, 8, 9))
    w_t[:256] = turned(w_inner[:, :256])
    gw_t[...] = turned(gate_weight[...])
    ow_t[...] = turned(out_weight[...])
    lax.fori_loop(0, 16, project_left, 0, unroll=4)
    pl.semaphore_wait(all_sem, 3)
    lax.fori_loop(1, 4, lambda dy, _: lax.fori_loop(0, 4, lambda dx, _: send_right(dx, dy), 0), 0)
    for role in range(2):
        recv_l[role * 64 + place] = channel(0, mine[role])
        recv_r[role * 64 + place] = channel(128, mine[role])
    send_left(2)

    def pass_copy(role):
        return pltpu.make_async_remote_copy(
            recv_r.at[pl.ds(role * 64, 64)], passed.at[pl.ds((1 - role) * 64, 64)],
            pass_send_sem.at[role], pass_recv_sem.at[1 - role],
            device_id=line("z", 7 if role else 1), device_id_type=MESH,
        )

    others = pl.ds(0, CHIPS - 2)
    pltpu.make_async_copy(recv_r.at[others], recv_r.at[others], recv_r_sem).wait()
    for role in range(2):
        pass_copy(role).start()
    for j in (3, 1, 0):
        send_left(j)

    def gates(r, _):
        g = jnp.dot(gw_t[...], normed[r], preferred_element_type=F32) + twice(cols[6])
        gate[r] = sigmoid(g)
        return 0

    lax.fori_loop(0, 16, gates, 0, unroll=2)

    def assemble(src, b, dst, at):
        for p in range(4):
            one, two = src[b * 8 + 2 * p], src[b * 8 + 2 * p + 1]
            k = slice(p * 128, p * 128 + 128)
            dst[pl.ds(at, 32), k] = jnp.concatenate([one[:, :64], two[:, :64]], axis=1)
            dst[pl.ds(at + 32, 32), k] = jnp.concatenate([one[:, 64:], two[:, 64:]], axis=1)

    def assemble_right(src, role, j, plane):
        for lo in range(2):
            at = role * 1024 + lax.rem(plane, 2) * 512 + (lo * 4 + lax.div(plane, 2)) * 64
            assemble(src, (role * 4 + j) * 2 + lo, right_m, pl.multiple_of(at, 64))

    def direct(j, _):
        assemble_right(recv_r, 0, j, lax.rem(z + 8 - j, 8))
        assemble_right(recv_r, 1, j, lax.rem(z + j, 8))
        return 0

    def indirect(j, _):
        assemble_right(passed, 0, j, lax.rem(z + 1 + j, 8))
        assemble_right(passed, 1, j, lax.rem(z + 7 - j, 8))
        return 0

    lax.fori_loop(0, 4, direct, 0)
    for role in range(2):
        ref = passed.at[pl.ds(role * 64, 64)]
        pltpu.make_async_copy(ref, ref, pass_recv_sem.at[role]).wait()
    lax.fori_loop(0, 4, indirect, 0)

    def part_copy(t, role):
        return pltpu.make_async_remote_copy(
            part_out.at[t, role], part_in.at[t, role], part_send_sem.at[t, role], part_recv_sem.at[t, role],
            device_id=sibling, device_id_type=MESH,
        )

    def product(role, half):
        rhs = right_m[pl.ds(pl.multiple_of(role * 1024 + half * 512, 512), 512), :]
        return lax.dot_general(left_m[role * 128 : role * 128 + 128], rhs, NT, preferred_element_type=F32)

    def multiply(t):
        some = pl.ds(0, 32 if t else 30)
        pltpu.make_async_copy(recv_l.at[some], recv_l.at[some], recv_l_sem.at[t]).wait()
        for role in range(2):
            for lo in range(2):
                assemble(recv_l, (role * 4 + t) * 2 + lo, left_m, role * 128 + lo * 64)
        for role in range(2):
            part_out[t, role] = product(role, 1 - core).astype(BF16)
            part_copy(t, role).start()
        for role in range(2):
            acc[role] = product(role, core)
        for role in range(2):
            part_copy(t, role).wait_recv()
            tri = (acc[role] + part_in[t, role].astype(F32)).astype(BF16)
            for lo in range(2):
                for kb in range(8):
                    low = tri[lo * 64 : lo * 64 + 32, kb * 64 : kb * 64 + 64]
                    high = tri[lo * 64 + 32 : lo * 64 + 64, kb * 64 : kb * 64 + 64]
                    send2[((role * 4 + t) * 2 + lo) * 8 + kb] = jnp.concatenate([low, high], axis=1)

        def give_back(step, half):
            part = slice(half * 16, half * 16 + 16)
            kb = lax.rem(col * 2 + x_hi + step, 8)
            y_to = lax.div(kb, 2)
            ka_to = lax.rem(kb, 2) * 2 + core
            for role in range(2):
                for lo in range(2):
                    tile = ((role * 4 + t) * 2 + lo) * 8 + kb
                    row_to = lo * 8 + z_at[t if role else (8 - t) % 8]
                    copy = pltpu.make_async_remote_copy(
                        send2.at[tile, part], recv2.at[mine[role], part], send2_sem, recv2_sem.at[half],
                        device_id=(row_to, y_to, ka_to), device_id_type=MESH,
                    )
                    if t:
                        copy.start()
                        continue
                    ours = kb * ROWS + row_to == me

                    @pl.when(ours)
                    def _():
                        recv2[mine[role], part] = send2[tile, part]

                    @pl.when(jnp.logical_not(ours))
                    def _():
                        copy.start()

            return 0

        for half in range(2):
            lax.fori_loop(0, 8, lambda step, _: give_back(step, half), 0)

    for t in (2, 3, 1, 0):
        multiply(t)

    def widen(half):
        def one(h, _):
            at = pl.multiple_of(h * 32 + half * 16, 16)
            flat[pl.ds(at, 16), :] = recv2[h, pl.ds(half * 16, 16)].astype(F32)
            return 0

        return one

    def finish(r, _):
        r0 = 2 * r
        t = jnp.concatenate(
            [flat[pl.ds(r0, 128, stride=32), :], flat[pl.ds(r0 + 1, 128, stride=32), :]], axis=1
        )
        n = normalise(t, twice(cols[7]), twice(cols[8])).astype(BF16)
        projected = jnp.dot(ow_t[...], n, preferred_element_type=F32) + twice(cols[9])
        update = (gate[r] * projected).T.astype(BF16)
        out[r0] = update[:64]
        out[r0 + 32] = update[64:128]
        out[r0 + 1] = update[128:192]
        out[r0 + 33] = update[192:]
        return 0

    for half in range(2):
        rows_in = recv2.at[others, pl.ds(half * 16, 16)]
        pltpu.make_async_copy(rows_in, rows_in, recv2_sem.at[half]).wait()
        lax.fori_loop(0, CHIPS, widen(half), 0, unroll=16)
        for c in (2 * half, 2 * half + 1):
            lax.fori_loop(4 * c, 4 * c + 4, finish, 0, unroll=4)
            for copy in quarter(out, out_hbm, out_sem, c):
                copy.start()

    pltpu.make_async_copy(send_l.at[others], send_l.at[others], send_l_sem).wait()
    pltpu.make_async_copy(send_r.at[others], send_r.at[others], send_r_sem).wait()
    pltpu.make_async_copy(send2.at[others], send2.at[others], send2_sem).wait()
    for role in range(2):
        pass_copy(role).wait_send()
        for t in range(4):
            part_copy(t, role).wait_send()
    for c in range(4):
        for copy in quarter(out, out_hbm, out_sem, c):
            copy.wait()


def on_device(pair, in_gain, in_shift, w_inner, inner_bias, gate_weight, gate_bias, out_gain, out_shift, out_weight, out_bias):
    anywhere = pl.BlockSpec(memory_space=pl.ANY)
    dma = pltpu.SemaphoreType.DMA
    as_row = lambda v: v.reshape(1, -1)
    return pl.pallas_call(
        kernel,
        out_shape=jax.ShapeDtypeStruct((64, 64, 128), BF16),
        in_specs=[anywhere] * 11,
        out_specs=anywhere,
        scratch_shapes=[
            *(pltpu.VMEM(shape, dtype) for shape, dtype in SMALL),
            pltpu.VMEM((64, 64, 128), BF16),
            pltpu.VMEM((64, 64, 128), BF16),
            dma((10,)), dma((4, 2)), dma((4, 2)), pltpu.SemaphoreType.REGULAR, pltpu.SemaphoreType.REGULAR,
            pltpu.VMEM((10, 128, 128), F32),
            pltpu.VMEM((512, 128), BF16),
            pltpu.VMEM((128, 128), BF16),
            pltpu.VMEM((128, 128), BF16),
            pltpu.VMEM((32 * 256, 128), F32),
            pltpu.VMEM((16, 128, 256), BF16),
            *[pltpu.VMEM((CHIPS, 32, 128), BF16)] * 5,
            pltpu.VMEM((256, 512), BF16),
            pltpu.VMEM((2048, 512), BF16),
            pltpu.VMEM((2, 128, 512), F32),
            *[pltpu.VMEM((4, 2, 128, 512), BF16)] * 2,
            *[pltpu.VMEM((CHIPS, 32, 128), BF16)] * 2,
            pltpu.VMEM((16, 128, 256), F32),
            dma, dma((4,)), dma, dma, dma((2,)), dma((2,)), dma((4, 2)), dma((4, 2)), dma, dma((2,)),
        ],
        compiler_params=pltpu.CompilerParams(
            collective_id=0, has_side_effects=True, vmem_limit_bytes=56 * 2**20
        ),
    )(
        pair, as_row(in_gain), as_row(in_shift), w_inner, as_row(inner_bias), gate_weight, as_row(gate_bias),
        as_row(out_gain), as_row(out_shift), out_weight, as_row(out_bias),
    )


def solution(mesh):
    placed = (P("row", ("col", "ka"), None),) + (P(),) * 10
    return jax.shard_map(
        on_device, mesh=mesh, in_specs=placed, out_specs=P("row", ("col", "ka"), None), check_vma=False
    )
```
